512 devices in a mesh: rep: 8 (over x, core), exp: 64 (over z, y).
Axes of the slice: x: 4, y: 8, z: 8, core: 2. Of those that a mesh axis runs over, the one named last changes fastest.
Arguments:
- hidden: bfloat16 [8, 64, 320, 768], P('rep', 'exp'), may hold values from -6 to 6
- down_weight: bfloat16 [64, 768, 4096], P('exp', None, 'rep'), may hold values from -0.21875 to 0.21875
- grad_out: bfloat16 [65536, 4096], P(('rep', 'exp')), may hold values from -6 to 6
- expert_ids: int32 [65536, 2], P(('rep', 'exp')), may hold values from 0 to 63, all different within a row; in each aligned block of 128 rows (0 to 127, 128 to 255, ...) at most 5 rows name the same one
- gate_weights: float32 [65536, 2], P(('rep', 'exp')), may hold values from 0.03 to 0.4
Outputs:
- combined: bfloat16 [65536, 4096], P(('rep', 'exp'))
- hidden_grad: bfloat16 [8, 64, 320, 768], P('rep', 'exp')
- weight_grad: bfloat16 [64, 768, 4096], P('exp', None, 'rep')
- gate_grad: float32 [65536, 2], P(('rep', 'exp'))
The draws below stay inside these ranges and needn't reach their ends.
Inputs may be any that keep to these rules, and one draw needn't show every extreme that they name: `expert_ids`: A token names 2 different experts. Within the 128 tokens of one device no expert is named more than 5 times, a bound that some block reaches.
All inputs are finite; a program needn't handle non-finite values.
Results may differ from the reference program's by a relative error of at most 0.014.
Values may be sent and summed in bfloat16 or wider, within the bound.
A program may use at most 64 MiB of HBM per device.

```python
import math
import jax
import jax.numpy as jnp
import numpy as np
from jax import lax

D = 4096
FF = 768
TOP = 2
TOK_DEV = 128
EXPERTS = 64
CAP = 5
TOKENS = 65536
N_REP = 8
N_EXP = 64


def block_levels(own_key, extent, split, least, high):
    gain, own = 1.0, jax.random.fold_in(own_key, 6)
    for dim, blocks in split:
        heights = jnp.exp(jax.random.uniform(jax.random.fold_in(own, dim), (blocks,), jnp.float32, least / len(split), high / len(split)))
        gain = gain * jnp.repeat(heights, extent[dim] // blocks).reshape([-1 if axis == dim else 1 for axis in range(len(extent))])
    return gain


def deal_out(key, own, number, rows, number_of, top, bound, lean):
    order = jax.random.permutation(key, number_of)
    packed, ordinary = shares(number_of, rows * top, bound, lean, True), shares(number_of, rows * top, bound, lean, False)
    places = jnp.arange(number_of)

    def named(lengths, turn):
        used = int((lengths > 0).sum())
        fixed = max(1, used // 4)
        shifted = fixed + (places - fixed + turn * (used - fixed)) % max(1, number_of - fixed)
        return jnp.zeros((number_of,), jnp.int32).at[order[jnp.where(places < fixed, places, shifted)]].set(jnp.asarray(lengths, jnp.int32))

    lengths = jnp.where(number % 4 == 0, named(packed, number // 4), named(ordinary, number - number // 4 - 1))
    mixed = jax.random.permutation(jax.random.fold_in(own, 3), number_of)
    donor, taker = mixed[0:number_of // 2 * 2:2], mixed[1:number_of // 2 * 2:2]
    room = jnp.minimum(lengths[donor] - 1, bound - lengths[taker]) // 2
    room = jnp.where((donor == order[0]) | (taker == order[0]) | (lengths[taker] == 0), 0, jnp.maximum(room, 0))
    shifted = jax.random.randint(jax.random.fold_in(own, 4), (number_of // 2,), 0, 1 << 20) % (room + 1)
    lengths = lengths.at[donor].add(-shifted).at[taker].add(shifted)
    labels = jnp.searchsorted(jnp.cumsum(lengths), jnp.arange(rows * top), side="right").astype(jnp.int32)
    listing = labels.reshape(top, rows).T
    listing = listing[jax.random.permutation(jax.random.fold_in(own, 1), rows)]
    turn = jax.random.randint(jax.random.fold_in(own, 2), (rows, 1), 0, top)
    return jnp.take_along_axis(listing, (jnp.arange(top)[None, :] + turn) % top, axis=1)


def shares(number_of, total, most, lean, full):
    loads = [(1 << 20) // math.isqrt(rank ** lean) + 1 for rank in range(1, number_of + 1)]
    largest = most if full else min(most, max(-(-total // number_of), total * loads[0] // sum(loads)))
    least = 1 if total - largest >= number_of - 1 else 0
    holding, spare = [largest] + [least] * (number_of - 1), total - largest - least * (number_of - 1)
    while spare > 0:
        free = [i for i in range(1, number_of) if holding[i] < largest] or [i for i in range(1, number_of) if holding[i] < most]
        pool, left = sum([loads[i] for i in free]), spare
        for i in free:
            addition = min(most - holding[i], max(1, left * loads[i] // pool), spare)
            holding[i] = holding[i] + addition
            spare = spare - addition
    return np.array(holding)


def bell_draw(stream_key, dims, spread, reach, cuts=(), held_as=jnp.bfloat16):
    entries = spread * jax.random.normal(stream_key, dims, jnp.float32)
    if cuts:
        entries = entries * block_levels(stream_key, dims, cuts, -0.22, 0.18)
    return jnp.clip(entries, -reach, reach).astype(held_as)


def setup_inputs(seed: int = 0) -> dict:
    key_list = jax.random.split(jax.random.key(seed), 6)
    hidden = bell_draw(key_list[0], (N_REP, EXPERTS, N_EXP * CAP, FF), 1.0, 6.0, ((0, 8), (1, 64)))
    down_weight = bell_draw(key_list[1], (EXPERTS, FF, D), FF ** -0.5, 0.21875, ((0, 64), (2, 8)))
    grad_out = bell_draw(key_list[2], (TOKENS, D), 1.0, 6.0, ((0, 512),))
    expert_ids_keys = jax.random.split(jax.random.fold_in(key_list[3], 1), TOKENS // TOK_DEV)
    expert_ids_turns = jax.random.permutation(jax.random.fold_in(key_list[3], 3), TOKENS // TOK_DEV)
    expert_ids = jax.vmap(lambda own, number: deal_out(jax.random.fold_in(key_list[3], 2), own, number, TOK_DEV, EXPERTS, TOP, CAP, 2))(expert_ids_keys, expert_ids_turns).reshape((TOKENS, TOP))
    gate_weights = jnp.clip(jnp.exp(math.log(0.4) - 2.5902672 * jax.random.uniform(key_list[4], (TOKENS, TOP), jnp.float32) ** block_levels(key_list[4], (TOKENS, TOP), ((0, 512),), -0.2, 0.2)), 0.03, 0.4)
    return dict(hidden=hidden, down_weight=down_weight, grad_out=grad_out, expert_ids=expert_ids, gate_weights=gate_weights)


def reference(hidden, down_weight, grad_out, expert_ids, gate_weights):
    slots_all = N_EXP * CAP
    slice_width = D // N_REP
    routed = expert_ids.reshape(N_REP, N_EXP, TOK_DEV, TOP)
    matches = (routed[..., None] == jnp.arange(EXPERTS, dtype=jnp.int32)).astype(jnp.int32)
    per_token = jnp.sum(matches, axis=3).astype(jnp.int32)
    before = (jnp.cumsum(per_token, axis=2) - per_token).astype(jnp.int32)
    position = jnp.sum(matches * before[:, :, :, None, :], axis=4).astype(jnp.int32)
    slot_index = (jnp.arange(N_EXP, dtype=jnp.int32)[None, :, None, None] * CAP + position).astype(jnp.int32)
    replica = jnp.broadcast_to(jnp.arange(N_REP, dtype=jnp.int32)[:, None, None, None], routed.shape)
    token_index = jnp.broadcast_to(jnp.arange(TOKENS, dtype=jnp.int32).reshape(N_REP, N_EXP, TOK_DEV, 1), routed.shape)
    token_table = jnp.zeros((N_REP, EXPERTS, slots_all), jnp.int32).at[replica, routed, slot_index].set(token_index)
    gate_table = jnp.zeros((N_REP, EXPERTS, slots_all), jnp.float32).at[replica, routed, slot_index].set(gate_weights.reshape(routed.shape))

    def one_expert(mixed_sum, inputs):
        slot_rows, weight, tokens, slot_gates = inputs
        expert_out = jnp.einsum("rnf,fd->rnd", slot_rows.astype(jnp.float32), weight.astype(jnp.float32)).astype(jnp.bfloat16)
        out_wide = expert_out.astype(jnp.float32)
        flat_tokens = tokens.reshape(-1)
        mixed_sum = mixed_sum.at[flat_tokens].add((slot_gates[..., None] * out_wide).reshape(-1, D))
        upstream = grad_out[tokens].astype(jnp.float32)
        scores = jnp.sum(upstream * out_wide, axis=2)
        slot_grad = (upstream * slot_gates[..., None]).astype(jnp.bfloat16)
        weight_part = jnp.einsum("rnf,rnd->fd", slot_rows.astype(jnp.float32), slot_grad.astype(jnp.float32)).astype(jnp.bfloat16)
        pieces = jnp.einsum("rnqd,fqd->rnqf", slot_grad.astype(jnp.float32).reshape(N_REP, slots_all, N_REP, slice_width), weight.astype(jnp.float32).reshape(FF, N_REP, slice_width)).astype(jnp.bfloat16)
        hidden_part = jnp.sum(pieces.astype(jnp.float32), axis=2).astype(jnp.bfloat16)
        return mixed_sum, (weight_part, hidden_part, scores)

    start_sum = jnp.zeros((TOKENS, D), jnp.float32)
    inputs = (jnp.swapaxes(hidden, 0, 1), down_weight, jnp.swapaxes(token_table, 0, 1), jnp.swapaxes(gate_table, 0, 1))
    mixed_sum, (weight_grad, hidden_parts, scores) = lax.scan(one_expert, start_sum, inputs)
    hidden_grad = jnp.swapaxes(hidden_parts, 0, 1)
    gate_grad = scores[routed, replica, slot_index].reshape(TOKENS, TOP)
    return (mixed_sum.astype(jnp.bfloat16), hidden_grad, weight_grad, gate_grad)
```

```python
import functools

import jax
import jax.numpy as jnp
from jax import lax
from jax.experimental import pallas as pl
from jax.experimental.pallas import tpu as pltpu
from jax.sharding import PartitionSpec as P

MESH = pl.DeviceIdType.MESH
BF16 = jnp.bfloat16
F32 = jnp.float32
TOK, D, FF, CAP, SIDE, NX = 128, 4096, 768, 5, 8, 4
SRC = SIDE * SIDE
SLOTS = SRC * CAP
REP = 8
BW = D // REP
LANES = 128
GROUPS = 16
CHUNKS = ((0, 2), (2, 5))


def dot(a, b, ca, cb):
    return lax.dot_general(a, b, (((ca,), (cb,)), ((), ())), preferred_element_type=F32)


def kernel(
    hid, w, grad, ids, gates, comb_o, hg_o, dw_o, gg_o,
    S, M, R, F, wf, sgb, hp, hpT, PT, PP, dws, sibr, xs, xr, acc, hacc,
    send, recv, loc, wsend, wrecv, wloc, dsend, drecv,
):
    r = lax.axis_index("rep")
    e = lax.axis_index("exp")
    z, y = e // SIDE, e % SIDE
    x, core = r // 2, r % 2
    sib = x * 2 + 1 - core

    def zdev(t):
        return (r, t * SIDE + y)

    def ydev(t):
        return (r, z * SIDE + t)

    def xdev(t):
        return (t * 2 + core, e)

    barrier = pltpu.get_barrier_semaphore()

    def greet(o, carry):
        pl.semaphore_signal(barrier, inc=1, device_id=zdev((z + o) % SIDE), device_id_type=MESH)
        pl.semaphore_signal(barrier, inc=1, device_id=ydev((y + o) % SIDE), device_id_type=MESH)
        return carry

    lax.fori_loop(1, SIDE, greet, 0)
    for o in range(1, NX):
        pl.semaphore_signal(barrier, inc=1, device_id=xdev((x + o) % NX), device_id_type=MESH)
    pl.semaphore_signal(barrier, inc=1, device_id=(sib, e), device_id_type=MESH)

    wcopy = pltpu.make_async_copy(w, wf.at[r], wloc)
    wcopy.start()

    def alternate(i, o):
        k = (o + 1) // 2
        return (i + SIDE + k * (2 * (o % 2) - 1)) % SIDE

    def pair(a, phase, h, c0, n, t):
        cs = pl.ds(c0, n)
        if phase == 0 and h == 0:
            return S.at[a, 0, cs, t], M.at[a, 0, cs, z]
        if phase == 0:
            return S.at[a, 1, cs, :, t], M.at[a, 1, cs, y]
        if h == 0:
            return M.at[a, 0, cs, :, t], R.at[a, 0, cs, :, y]
        return M.at[a, 1, cs, :, t], R.at[a, 1, cs, z]

    def start_phase(a, phase, h, ch):
        c0, c1 = CHUNKS[ch]
        n = c1 - c0
        along_z = (phase == 0) == (h == 0)
        me = z if along_z else y

        def one(o, carry):
            t = alternate(me, o)
            s, d = pair(a, phase, h, c0, n, t)
            pltpu.make_async_remote_copy(
                src_ref=s, dst_ref=d,
                send_sem=send.at[a, phase, h], recv_sem=recv.at[a, phase, h, ch],
                device_id=zdev(t) if along_z else ydev(t), device_id_type=MESH,
            ).start()
            return carry

        lax.fori_loop(1, SIDE, one, 0)
        s, d = pair(a, phase, h, c0, n, me)
        pltpu.make_async_copy(s, d, loc.at[a, phase, h, ch]).start()

    def wait_phase(a, phase, h, ch):
        c0, c1 = CHUNKS[ch]
        n = c1 - c0
        me = z if (phase == 0) == (h == 0) else y
        s, d = pair(a, phase, h, c0, n, me)
        pltpu.make_async_copy(s, d, loc.at[a, phase, h, ch]).wait()
        land = (M if phase == 0 else R).at[a, h, pl.ds(c0, n), pl.ds(0, SIDE - 1)]
        pltpu.make_async_copy(land, land, recv.at[a, phase, h, ch]).wait()

    def wait_sent(a, phase, h):
        part = (S if phase == 0 else M).at[a, h, :, pl.ds(0, SIDE - 1)]
        pltpu.make_async_copy(part, part, send.at[a, phase, h]).wait()

    def spread(a, h):
        def one(c, carry):
            rows = F[pl.ds(pl.multiple_of(c * SRC * GROUPS, SRC * GROUPS), SRC * GROUPS), :]
            S[a, h, c] = rows.astype(BF16).reshape(SIDE, SIDE, GROUPS, LANES)
            return carry
        lax.fori_loop(0, CAP, one, 0)

    def stash(b, value):
        for j in range(BW // LANES):
            g = (b % 4) * (BW // LANES) + j
            F[pl.ds(g, SLOTS, stride=GROUPS), :] = value[:, j * LANES:(j + 1) * LANES]

    def collect(a, h, c):
        F[pl.ds(0, SRC * GROUPS), :] = R[a, h, c].reshape(SRC * GROUPS, LANES).astype(F32)
        rows = pl.ds(pl.multiple_of(c * SRC, SRC), SRC)
        for g in range(GROUPS):
            part = F[pl.ds(g, SRC, stride=GROUPS), :].astype(BF16)
            j = g % (BW // LANES)
            sgb[h * 4 + g // (BW // LANES), rows, pl.ds(j * LANES, LANES)] = part

    lane = lax.broadcasted_iota(jnp.int32, (TOK, SRC), 1)
    m0 = (ids[:, 0:1] == lane).astype(F32)
    m1 = (ids[:, 1:2] == lane).astype(F32)
    earlier = (
        lax.broadcasted_iota(jnp.int32, (TOK, TOK), 1) < lax.broadcasted_iota(jnp.int32, (TOK, TOK), 0)
    ).astype(F32).astype(BF16)
    before = dot(earlier, (m0 + m1).astype(BF16), 1, 0)
    slot_lane = lax.broadcasted_iota(jnp.int32, (TOK, SLOTS), 1)
    for k, m in ((0, m0), (1, m1)):
        position = jnp.sum(m * before, axis=1, keepdims=True).astype(jnp.int32)
        target = position * SRC + ids[:, k:k + 1]
        PP[k * TOK:(k + 1) * TOK, :] = (slot_lane == target).astype(F32).astype(BF16)
    eye = (
        lax.broadcasted_iota(jnp.int32, (2 * TOK, 2 * TOK), 0)
        == lax.broadcasted_iota(jnp.int32, (2 * TOK, 2 * TOK), 1)
    ).astype(F32).astype(BF16)
    PT[...] = dot(PP[...], eye, 0, 0).astype(BF16)
    g0, g1 = gates[:, 0:1], gates[:, 1:2]

    def gather(b, carry):
        cols = pl.ds(pl.multiple_of(b * BW, BW), BW)
        part = grad[:, cols].astype(F32)
        scaled = jnp.concatenate([(g0 * part).astype(BF16), (g1 * part).astype(BF16)], axis=0)
        stash(b, dot(PT[...], scaled, 1, 0))
        return carry

    for h in range(2):
        lax.fori_loop(4 * h, 4 * h + 4, gather, 0)
        spread(0, h)
        if h == 0:
            pl.semaphore_wait(barrier, 2 * (SIDE - 1) + NX)
        for ch in range(len(CHUNKS)):
            start_phase(0, 0, h, ch)
    wcopy.wait()

    def wmove(b, dev, i):
        return pltpu.make_async_remote_copy(
            src_ref=wf.at[b], dst_ref=wf.at[b], send_sem=wsend.at[i], recv_sem=wrecv.at[i],
            device_id=dev, device_id_type=MESH,
        )

    wx = [wmove(r, xdev((x + o) % NX), o) for o in (1, 3, 2)]
    for c in wx:
        c.start()
    wsib = [wmove(r, (sib, e), 4)]
    wsib[0].start()

    row = lax.broadcasted_iota(jnp.int32, (SLOTS, SLOTS), 0)
    col = lax.broadcasted_iota(jnp.int32, (SLOTS, SLOTS), 1)
    perm = (col == (row % SRC) * CAP + row // SRC).astype(F32).astype(BF16)
    hp[...] = dot(perm, hid[...], 1, 0).astype(BF16)
    hpT[...] = dot(hid[...], perm, 0, 1).astype(BF16)

    for ch in range(len(CHUNKS)):
        for h in range(2):
            wait_phase(0, 0, h, ch)
            start_phase(0, 1, h, ch)

    for c, o in zip(wx, (1, 3, 2)):
        c.wait()
        fwd = wmove(((x + NX - o) % NX) * 2 + core, (sib, e), 4 + o)
        fwd.start()
        wsib.append(fwd)
    for c in wsib:
        c.wait()

    def expert(b, carry):
        stash(b, dot(hp[...], wf[b], 1, 0))
        return carry

    for h in range(2):
        lax.fori_loop(4 * h, 4 * h + 4, expert, 0)
        spread(1, h)
        for ch in range(len(CHUNKS)):
            start_phase(1, 0, h, ch)

    for ch, (c0, c1) in enumerate(CHUNKS):
        for h in range(2):
            wait_phase(0, 1, h, ch)

            def take(c, carry, h=h):
                collect(0, h, c)
                return carry

            lax.fori_loop(c0, c1, take, 0)

    def dmove(src, dst, dev, i):
        return pltpu.make_async_remote_copy(
            src_ref=src, dst_ref=dst, send_sem=dsend.at[i], recv_sem=drecv.at[i],
            device_id=dev, device_id_type=MESH,
        )

    def block_grad(b):
        return dot(hpT[...], sgb[b], 1, 0)

    def for_sibling(i, carry):
        dws[i] = block_grad(i * 2 + 1 - core).astype(BF16)
        dmove(dws.at[i], sibr.at[i], (sib, e), i).start()
        return carry

    lax.fori_loop(0, NX, for_sibling, 0)

    def back(b, carry):
        hacc[...] += dot(sgb[b], wf[b], 1, 1)
        return carry

    hacc[...] = jnp.zeros_like(hacc)
    lax.fori_loop(0, REP, back, 0)
    hg_o[...] = dot(perm, hacc[...].astype(BF16), 0, 0).astype(BF16)

    def own_type(o, carry):
        t = (x + o) % NX
        dmove(dws.at[t], sibr.at[t], (sib, e), t).wait()
        xs[o] = (block_grad(t * 2 + core) + sibr[t].astype(F32)).astype(BF16)
        dmove(xs.at[o], xr.at[o], xdev(t), NX + o).start()
        return carry

    lax.fori_loop(1, NX, own_type, 0)
    dmove(dws.at[x], sibr.at[x], (sib, e), x).wait()
    acc[...] = block_grad(r) + sibr[x].astype(F32)

    for ch in range(len(CHUNKS)):
        for h in range(2):
            wait_phase(1, 0, h, ch)
            start_phase(1, 1, h, ch)

    for o in (1, 3, 2):
        dmove(xs.at[o], xr.at[o], xdev((x + o) % NX), NX + o).wait()
    dw_o[...] = (acc[...] + xr[1].astype(F32) + xr[2].astype(F32) + xr[3].astype(F32)).astype(BF16)

    for ch, (c0, c1) in enumerate(CHUNKS):
        for h in range(2):
            wait_phase(1, 1, h, ch)

            def take(c, carry, h=h):
                collect(1, h, c)
                return carry

            lax.fori_loop(c0, c1, take, 0)

    def combine(b, carry):
        s0, s1 = carry
        cols = pl.ds(pl.multiple_of(b * BW, BW), BW)
        part = grad[:, cols].astype(F32)
        p0 = dot(PP[0:TOK, :], sgb[b], 1, 0)
        p1 = dot(PP[TOK:2 * TOK, :], sgb[b], 1, 0)
        comb_o[:, cols] = (g0 * p0 + g1 * p1).astype(BF16)
        return s0 + part * p0, s1 + part * p1

    zero = jnp.zeros((TOK, BW), F32)
    s0, s1 = lax.fori_loop(0, REP, combine, (zero, zero))
    gg_o[:, 0:1] = jnp.sum(s0, axis=1, keepdims=True)
    gg_o[:, 1:2] = jnp.sum(s1, axis=1, keepdims=True)

    for a in range(2):
        for phase in range(2):
            for h in range(2):
                wait_sent(a, phase, h)


def per_device(hidden, down_weight, grad_out, expert_ids, gate_weights):
    vmem = pl.BlockSpec(memory_space=pltpu.VMEM)
    dma = pltpu.SemaphoreType.DMA
    n = len(CHUNKS)
    a2a = pltpu.VMEM((2, 2, CAP, SIDE, SIDE, GROUPS, LANES), BF16)
    quarter = pltpu.VMEM((NX, FF, BW), BF16)
    combined, hidden_grad, weight_grad, gate_grad = pl.pallas_call(
        kernel,
        out_shape=(
            jax.ShapeDtypeStruct((TOK, D), BF16),
            jax.ShapeDtypeStruct((SLOTS, FF), BF16),
            jax.ShapeDtypeStruct((FF, BW), BF16),
            jax.ShapeDtypeStruct((TOK, 2), F32),
        ),
        in_specs=[vmem] * 5,
        out_specs=(vmem,) * 4,
        scratch_shapes=[
            a2a, a2a, a2a,
            pltpu.VMEM((SLOTS * GROUPS, LANES), F32),
            pltpu.VMEM((REP, FF, BW), BF16),
            pltpu.VMEM((REP, SLOTS, BW), BF16),
            pltpu.VMEM((SLOTS, FF), BF16),
            pltpu.VMEM((FF, SLOTS), BF16),
            pltpu.VMEM((SLOTS, 2 * TOK), BF16),
            pltpu.VMEM((2 * TOK, SLOTS), BF16),
            quarter, quarter, quarter, quarter,
            pltpu.VMEM((FF, BW), F32),
            pltpu.VMEM((SLOTS, FF), F32),
            dma((2, 2, 2)), dma((2, 2, 2, n)), dma((2, 2, 2, n)),
            dma((8,)), dma((8,)), dma,
            dma((8,)), dma((8,)),
        ],
        compiler_params=pltpu.CompilerParams(
            collective_id=0, has_side_effects=True, vmem_limit_bytes=60 * 1024 * 1024
        ),
        cost_estimate=pl.CostEstimate(
            flops=7_000_000_000, bytes_accessed=5_000_000, transcendentals=0
        ),
    )(hidden[0, 0], down_weight[0], grad_out, expert_ids, gate_weights)
    return combined, hidden_grad[None, None], weight_grad[None], gate_grad


def solution(mesh):
    return jax.shard_map(
        per_device,
        mesh=mesh,
        in_specs=(
            P("rep", "exp", None, None),
            P("exp", None, "rep"),
            P(("rep", "exp"), None),
            P(("rep", "exp"), None),
            P(("rep", "exp"), None),
        ),
        out_specs=(
            P(("rep", "exp"), None),
            P("rep", "exp", None, None),
            P("exp", None, "rep"),
            P(("rep", "exp"), None),
        ),
        check_vma=False,
    )
```

```python
import functools

import jax
import jax.numpy as jnp
from jax import lax
from jax.experimental import pallas as pl
from jax.experimental.pallas import tpu as pltpu
from jax.sharding import PartitionSpec as P

MESH = pl.DeviceIdType.MESH
BF16 = jnp.bfloat16
F32 = jnp.float32
TOK, D, FF, CAP, SIDE, NX = 128, 4096, 768, 5, 8, 4
SRC = SIDE * SIDE
SLOTS = SRC * CAP
REP = 8
BW = D // REP
LANES = 128
GROUPS = 16
CHUNKS = ((0, 2), (2, 4), (4, 5))
ORDER = ((0, 0), (1, 0), (0, 1), (1, 1), (0, 2), (1, 2))


def dot(a, b, ca, cb):
    return lax.dot_general(a, b, (((ca,), (cb,)), ((), ())), preferred_element_type=F32)


def kernel(
    hid, w, grad_in, ids, gates, comb_o, hg_o, dw_o, gg_o,
    S, M, R, F, wf, sgb, grad, hv, hp, hpT, PT, PP, dws, sibr, xs, xr, acc, hacc, gcol, gsum, pacc,
    send, recv, loc, wsend, wrecv, wloc, hloc, gloc, dsend, drecv,
):
    r = lax.axis_index("rep")
    e = lax.axis_index("exp")
    z, y = e // SIDE, e % SIDE
    x, core = r // 2, r % 2
    sib = x * 2 + 1 - core

    def zdev(t):
        return (r, t * SIDE + y)

    def ydev(t):
        return (r, z * SIDE + t)

    def xdev(t):
        return (t * 2 + core, e)

    barrier = pltpu.get_barrier_semaphore()

    def greet(o, carry):
        pl.semaphore_signal(barrier, inc=1, device_id=zdev((z + o) % SIDE), device_id_type=MESH)
        pl.semaphore_signal(barrier, inc=1, device_id=ydev((y + o) % SIDE), device_id_type=MESH)
        return carry

    lax.fori_loop(1, SIDE, greet, 0)
    for o in range(1, NX):
        pl.semaphore_signal(barrier, inc=1, device_id=xdev((x + o) % NX), device_id_type=MESH)
    pl.semaphore_signal(barrier, inc=1, device_id=(sib, e), device_id_type=MESH)

    gcopy = pltpu.make_async_copy(grad_in, grad, gloc)
    gcopy.start()
    wcopy = pltpu.make_async_copy(w, wf.at[r], wloc)
    wcopy.start()
    hcopy = pltpu.make_async_copy(hid, hv, hloc)
    hcopy.start()

    def alternate(i, o):
        k = (o + 1) // 2
        return (i + SIDE + k * (2 * (o % 2) - 1)) % SIDE

    def pair(a, phase, h, c0, n, t):
        cs = pl.ds(c0, n)
        if phase == 0 and h == 0:
            return S.at[a, 0, cs, t], M.at[a, 0, cs, z]
        if phase == 0:
            return S.at[a, 1, cs, :, t], M.at[a, 1, cs, y]
        if h == 0:
            return M.at[a, 0, cs, :, t], R.at[a, 0, cs, :, y]
        return M.at[a, 1, cs, :, t], R.at[a, 1, cs, z]

    def start_phase(a, phase, h, ch):
        c0, c1 = CHUNKS[ch]
        n = c1 - c0
        along_z = (phase == 0) == (h == 0)
        me = z if along_z else y

        def one(o, carry):
            t = alternate(me, o)
            s, d = pair(a, phase, h, c0, n, t)
            pltpu.make_async_remote_copy(
                src_ref=s, dst_ref=d,
                send_sem=send.at[a, phase, h], recv_sem=recv.at[a, phase, h, ch],
                device_id=zdev(t) if along_z else ydev(t), device_id_type=MESH,
            ).start()
            return carry

        lax.fori_loop(1, SIDE, one, 0)
        s, d = pair(a, phase, h, c0, n, me)
        pltpu.make_async_copy(s, d, loc.at[a, phase, h, ch]).start()

    def wait_phase(a, phase, h, ch):
        c0, c1 = CHUNKS[ch]
        n = c1 - c0
        me = z if (phase == 0) == (h == 0) else y
        s, d = pair(a, phase, h, c0, n, me)
        pltpu.make_async_copy(s, d, loc.at[a, phase, h, ch]).wait()
        land = (M if phase == 0 else R).at[a, h, pl.ds(c0, n), pl.ds(0, SIDE - 1)]
        pltpu.make_async_copy(land, land, recv.at[a, phase, h, ch]).wait()

    def wait_sent(a, phase, h):
        part = (S if phase == 0 else M).at[a, h, :, pl.ds(0, SIDE - 1)]
        pltpu.make_async_copy(part, part, send.at[a, phase, h]).wait()

    def spread(a, h):
        def one(c, carry):
            rows = F[pl.ds(pl.multiple_of(c * SRC * GROUPS, SRC * GROUPS), SRC * GROUPS), :]
            S[a, h, c] = rows.astype(BF16).reshape(SIDE, SIDE, GROUPS, LANES)
            return carry
        lax.fori_loop(0, CAP, one, 0)

    def stash(b, value):
        for j in range(BW // LANES):
            g = (b % 4) * (BW // LANES) + j
            F[pl.ds(g, SLOTS, stride=GROUPS), :] = value[:, j * LANES:(j + 1) * LANES]

    def collect(a, h, c):
        F[pl.ds(0, SRC * GROUPS), :] = R[a, h, c].reshape(SRC * GROUPS, LANES).astype(F32)
        rows = pl.ds(pl.multiple_of(c * SRC, SRC), SRC)
        for g in range(GROUPS):
            part = F[pl.ds(g, SRC, stride=GROUPS), :].astype(BF16)
            j = g % (BW // LANES)
            sgb[h * 4 + g // (BW // LANES), rows, pl.ds(j * LANES, LANES)] = part

    expert_row = lax.broadcasted_iota(jnp.int32, (SRC, TOK), 0)
    m0 = (ids[0:1, :] == expert_row).astype(F32)
    m1 = (ids[1:2, :] == expert_row).astype(F32)
    earlier = (
        lax.broadcasted_iota(jnp.int32, (TOK, TOK), 0) < lax.broadcasted_iota(jnp.int32, (TOK, TOK), 1)
    ).astype(F32).astype(BF16)
    before = dot((m0 + m1).astype(BF16), earlier, 1, 0)
    slot_row = lax.broadcasted_iota(jnp.int32, (SLOTS, TOK), 0)
    for k, m in ((0, m0), (1, m1)):
        position = jnp.sum(m * before, axis=0, keepdims=True).astype(jnp.int32)
        target = position * SRC + ids[k:k + 1, :]
        PT[:, k * TOK:(k + 1) * TOK] = (slot_row == target).astype(F32).astype(BF16)
        gcol[k] = jnp.broadcast_to(gates[k:k + 1, :], (TOK, TOK)).T

    def gate(k):
        return jnp.concatenate([gcol[k]] * (BW // LANES), axis=1)

    def gather(b, carry):
        cols = pl.ds(pl.multiple_of(b * BW, BW), BW)
        part = grad[:, cols].astype(F32)
        scaled = jnp.concatenate([(gate(0) * part).astype(BF16), (gate(1) * part).astype(BF16)], axis=0)
        stash(b, dot(PT[...], scaled, 1, 0))
        return carry

    gcopy.wait()
    for h in range(2):
        lax.fori_loop(4 * h, 4 * h + 4, gather, 0)
        spread(0, h)
        if h == 0:
            pl.semaphore_wait(barrier, 2 * (SIDE - 1) + NX)
        for ch in range(len(CHUNKS)):
            start_phase(0, 0, h, ch)
    wcopy.wait()

    def wmove(b, dev, i):
        return pltpu.make_async_remote_copy(
            src_ref=wf.at[b], dst_ref=wf.at[b], send_sem=wsend.at[i], recv_sem=wrecv.at[i],
            device_id=dev, device_id_type=MESH,
        )

    wx = [wmove(r, xdev((x + o) % NX), o) for o in (1, 3, 2)]
    for c in wx:
        c.start()
    wsib = [wmove(r, (sib, e), 4)]
    wsib[0].start()

    eye = (
        lax.broadcasted_iota(jnp.int32, (SLOTS, SLOTS), 0)
        == lax.broadcasted_iota(jnp.int32, (SLOTS, SLOTS), 1)
    ).astype(F32).astype(BF16)
    PP[...] = dot(PT[...], eye, 0, 0).astype(BF16)
    hcopy.wait()
    row = lax.broadcasted_iota(jnp.int32, (SLOTS, SLOTS), 0)
    col = lax.broadcasted_iota(jnp.int32, (SLOTS, SLOTS), 1)
    perm = (col == (row % SRC) * CAP + row // SRC).astype(F32).astype(BF16)
    hp[...] = dot(perm, hv[...], 1, 0).astype(BF16)
    hpT[...] = dot(hv[...], perm, 0, 1).astype(BF16)

    for h, ch in ORDER:
        wait_phase(0, 0, h, ch)
        start_phase(0, 1, h, ch)

    for c, o in zip(wx, (1, 3, 2)):
        c.wait()
        fwd = wmove(((x + NX - o) % NX) * 2 + core, (sib, e), 4 + o)
        fwd.start()
        wsib.append(fwd)
    for c in wsib:
        c.wait()

    def expert(b, carry):
        stash(b, dot(hp[...], wf[b], 1, 0))
        return carry

    for h in range(2):
        lax.fori_loop(4 * h, 4 * h + 4, expert, 0)
        spread(1, h)
        for ch in range(len(CHUNKS)):
            start_phase(1, 0, h, ch)

    def take_in(a, h, ch):
        wait_phase(a, 1, h, ch)

        def take(c, carry):
            collect(a, h, c)
            return carry

        lax.fori_loop(*CHUNKS[ch], take, 0)

    for h, ch in ORDER:
        take_in(0, h, ch)

    def dmove(src, dst, dev, i):
        return pltpu.make_async_remote_copy(
            src_ref=src, dst_ref=dst, send_sem=dsend.at[i], recv_sem=drecv.at[i],
            device_id=dev, device_id_type=MESH,
        )

    def block_grad(b):
        return dot(hpT[...], sgb[b], 1, 0)

    def for_sibling(i, carry):
        dws[i] = block_grad(i * 2 + 1 - core).astype(BF16)
        dmove(dws.at[i], sibr.at[i], (sib, e), i).start()
        return carry

    lax.fori_loop(0, NX, for_sibling, 0)

    def back(b, carry):
        hacc[...] += dot(sgb[b], wf[b], 1, 1)
        return carry

    hacc[...] = jnp.zeros_like(hacc)
    lax.fori_loop(0, REP, back, 0)
    hg_o[...] = dot(perm, hacc[...].astype(BF16), 0, 0).astype(BF16)

    def own_type(o, carry):
        t = (x + o) % NX
        dmove(dws.at[t], sibr.at[t], (sib, e), t).wait()
        xs[o] = (block_grad(t * 2 + core) + sibr[t].astype(F32)).astype(BF16)
        dmove(xs.at[o], xr.at[o], xdev(t), NX + o).start()
        return carry

    lax.fori_loop(1, NX, own_type, 0)
    dmove(dws.at[x], sibr.at[x], (sib, e), x).wait()
    acc[...] = block_grad(r) + sibr[x].astype(F32)

    for h, ch in ORDER:
        wait_phase(1, 0, h, ch)
        start_phase(1, 1, h, ch)

    for o in (1, 3, 2):
        dmove(xs.at[o], xr.at[o], xdev((x + o) % NX), NX + o).wait()
    dw_o[...] = (acc[...] + xr[1].astype(F32) + xr[2].astype(F32) + xr[3].astype(F32)).astype(BF16)

    gsum[...] = jnp.zeros_like(gsum)
    last = len(CHUNKS) - 1
    for h, ch in ORDER:
        take_in(1, h, ch)
        rows = slice(CHUNKS[ch][0] * SRC, CHUNKS[ch][1] * SRC)

        def combine(b, carry, ch=ch, rows=rows):
            picked = dot(PP[:, rows], sgb[b, rows], 1, 0)
            if ch > 0:
                picked += pacc[b]
            if ch < last:
                pacc[b] = picked
                return carry
            cols = pl.ds(pl.multiple_of(b * BW, BW), BW)
            part = grad[:, cols].astype(F32)
            p0, p1 = picked[:TOK], picked[TOK:]
            comb_o[:, cols] = (gate(0) * p0 + gate(1) * p1).astype(BF16)
            for k, p in ((0, p0), (1, p1)):
                q = part * p
                gsum[k] += (q[:, 0:LANES] + q[:, LANES:2 * LANES]) + (
                    q[:, 2 * LANES:3 * LANES] + q[:, 3 * LANES:]
                )
            return carry

        lax.fori_loop(4 * h, 4 * h + 4, combine, 0)
    for k in range(2):
        gg_o[k:k + 1, :] = jnp.sum(gsum[k].T, axis=0, keepdims=True)

    for a in range(2):
        for phase in range(2):
            for h in range(2):
                wait_sent(a, phase, h)


def per_device(hidden, down_weight, grad_out, expert_ids, gate_weights):
    vmem = pl.BlockSpec(memory_space=pltpu.VMEM)
    hbm = pl.BlockSpec(memory_space=pl.ANY)
    dma = pltpu.SemaphoreType.DMA
    n = len(CHUNKS)
    a2a = pltpu.VMEM((2, 2, CAP, SIDE, SIDE, GROUPS, LANES), BF16)
    quarter = pltpu.VMEM((NX, FF, BW), BF16)
    combined, hidden_grad, weight_grad, gate_grad = pl.pallas_call(
        kernel,
        out_shape=(
            pltpu.VMEM((TOK, D), BF16),
            pltpu.VMEM((SLOTS, FF), BF16),
            pltpu.VMEM((FF, BW), BF16),
            pltpu.VMEM((2, TOK), F32),
        ),
        in_specs=[hbm, hbm, hbm, vmem, vmem],
        out_specs=(vmem,) * 4,
        scratch_shapes=[
            a2a, a2a, a2a,
            pltpu.VMEM((SLOTS * GROUPS, LANES), F32),
            pltpu.VMEM((REP, FF, BW), BF16),
            pltpu.VMEM((REP, SLOTS, BW), BF16),
            pltpu.VMEM((TOK, D), BF16),
            pltpu.VMEM((SLOTS, FF), BF16),
            pltpu.VMEM((SLOTS, FF), BF16),
            pltpu.VMEM((FF, SLOTS), BF16),
            pltpu.VMEM((SLOTS, 2 * TOK), BF16),
            pltpu.VMEM((2 * TOK, SLOTS), BF16),
            quarter, quarter, quarter, quarter,
            pltpu.VMEM((FF, BW), F32),
            pltpu.VMEM((SLOTS, FF), F32),
            pltpu.VMEM((2, TOK, LANES), F32),
            pltpu.VMEM((2, TOK, LANES), F32),
            pltpu.VMEM((REP, 2 * TOK, BW), F32),
            dma((2, 2, 2)), dma((2, 2, 2, n)), dma((2, 2, 2, n)),
            dma((8,)), dma((8,)), dma, dma, dma,
            dma((8,)), dma((8,)),
        ],
        compiler_params=pltpu.CompilerParams(
            collective_id=0, has_side_effects=True, vmem_limit_bytes=57 * 1024 * 1024
        ),
        cost_estimate=pl.CostEstimate(
            flops=7_000_000_000, bytes_accessed=5_000_000, transcendentals=0
        ),
    )(hidden[0, 0], down_weight[0], grad_out, expert_ids.T, gate_weights.T)
    return combined, hidden_grad[None, None], weight_grad[None], gate_grad.T


def solution(mesh):
    return jax.shard_map(
        per_device,
        mesh=mesh,
        in_specs=(
            P("rep", "exp", None, None),
            P("exp", None, "rep"),
            P(("rep", "exp"), None),
            P(("rep", "exp"), None),
            P(("rep", "exp"), None),
        ),
        out_specs=(
            P(("rep", "exp"), None),
            P("rep", "exp", None, None),
            P("exp", None, "rep"),
            P(("rep", "exp"), None),
        ),
        check_vma=False,
    )
```

```python
import functools

import jax
import jax.numpy as jnp
from jax import lax
from jax.experimental import pallas as pl
from jax.experimental.pallas import tpu as pltpu
from jax.sharding import PartitionSpec as P

MESH = pl.DeviceIdType.MESH
BF16 = jnp.bfloat16
F32 = jnp.float32
TOK, D, FF, CAP, SIDE, NX = 128, 4096, 768, 5, 8, 4
SRC = SIDE * SIDE
SLOTS = SRC * CAP
REP = 8
BW = D // REP
LANES = 128
GROUPS = 16
CHUNKS = ((0, 2), (2, 4), (4, 5))
ORDER = ((0, 0), (1, 0), (0, 1), (1, 1), (0, 2), (1, 2))


def dot(a, b, ca, cb):
    return lax.dot_general(a, b, (((ca,), (cb,)), ((), ())), preferred_element_type=F32)


def kernel(
    hid, w, grad_in, ids, gates, comb_o, hg_o, dw_o, gg_o,
    S, M, R, F, wf, sgb, grad, hv, hp, hpT, PT, PP, dws, sibr, xs, xr, acc, hacc, gcol, gsum, pacc,
    send, recv, loc, wsend, wrecv, wloc, hloc, gloc, dsend, drecv,
):
    r = lax.axis_index("rep")
    e = lax.axis_index("exp")
    z, y = e // SIDE, e % SIDE
    x, core = r // 2, r % 2
    sib = x * 2 + 1 - core

    def zdev(t):
        return (r, t * SIDE + y)

    def ydev(t):
        return (r, z * SIDE + t)

    def xdev(t):
        return (t * 2 + core, e)

    barrier = pltpu.get_barrier_semaphore()

    def greet(o, carry):
        pl.semaphore_signal(barrier, inc=1, device_id=zdev((z + o) % SIDE), device_id_type=MESH)
        pl.semaphore_signal(barrier, inc=1, device_id=ydev((y + o) % SIDE), device_id_type=MESH)
        return carry

    lax.fori_loop(1, SIDE, greet, 0)
    for o in range(1, NX):
        pl.semaphore_signal(barrier, inc=1, device_id=xdev((x + o) % NX), device_id_type=MESH)
    pl.semaphore_signal(barrier, inc=1, device_id=(sib, e), device_id_type=MESH)

    gcopy = pltpu.make_async_copy(grad_in, grad, gloc)
    gcopy.start()
    wcopy = pltpu.make_async_copy(w, wf.at[r], wloc)
    wcopy.start()
    hcopy = pltpu.make_async_copy(hid, hv, hloc)
    hcopy.start()

    def alternate(i, o):
        k = (o + 1) // 2
        return (i + SIDE + k * (2 * (o % 2) - 1)) % SIDE

    def pair(a, phase, h, c0, n, t):
        cs = pl.ds(c0, n)
        if phase == 0 and h == 0:
            return S.at[a, 0, cs, t], M.at[a, 0, cs, z]
        if phase == 0:
            return S.at[a, 1, cs, :, t], M.at[a, 1, cs, y]
        if h == 0:
            return M.at[a, 0, cs, :, t], R.at[a, 0, cs, :, y]
        return M.at[a, 1, cs, :, t], R.at[a, 1, cs, z]

    def start_phase(a, phase, h, ch):
        c0, c1 = CHUNKS[ch]
        n = c1 - c0
        along_z = (phase == 0) == (h == 0)
        me = z if along_z else y

        def one(o, carry):
            t = alternate(me, o)
            s, d = pair(a, phase, h, c0, n, t)
            pltpu.make_async_remote_copy(
                src_ref=s, dst_ref=d,
                send_sem=send.at[a, phase, h], recv_sem=recv.at[a, phase, h, ch],
                device_id=zdev(t) if along_z else ydev(t), device_id_type=MESH,
            ).start()
            return carry

        lax.fori_loop(1, SIDE, one, 0)
        s, d = pair(a, phase, h, c0, n, me)
        pltpu.make_async_copy(s, d, loc.at[a, phase, h, ch]).start()

    def wait_phase(a, phase, h, ch):
        c0, c1 = CHUNKS[ch]
        n = c1 - c0
        me = z if (phase == 0) == (h == 0) else y
        s, d = pair(a, phase, h, c0, n, me)
        pltpu.make_async_copy(s, d, loc.at[a, phase, h, ch]).wait()
        land = (M if phase == 0 else R).at[a, h, pl.ds(c0, n), pl.ds(0, SIDE - 1)]
        pltpu.make_async_copy(land, land, recv.at[a, phase, h, ch]).wait()

    def wait_sent(a, phase, h):
        part = (S if phase == 0 else M).at[a, h, :, pl.ds(0, SIDE - 1)]
        pltpu.make_async_copy(part, part, send.at[a, phase, h]).wait()

    def spread(a, h):
        def one(c, carry):
            rows = F[pl.ds(pl.multiple_of(c * SRC * GROUPS, SRC * GROUPS), SRC * GROUPS), :]
            S[a, h, c] = rows.astype(BF16).reshape(SIDE, SIDE, GROUPS, LANES)
            return carry
        lax.fori_loop(0, CAP, one, 0)

    def stash(b, value):
        for j in range(BW // LANES):
            g = (b % 4) * (BW // LANES) + j
            F[pl.ds(g, SLOTS, stride=GROUPS), :] = value[:, j * LANES:(j + 1) * LANES]

    def collect(a, h, c):
        F[pl.ds(0, SRC * GROUPS), :] = R[a, h, c].reshape(SRC * GROUPS, LANES).astype(F32)
        rows = pl.ds(pl.multiple_of(c * SRC, SRC), SRC)
        for g in range(GROUPS):
            part = F[pl.ds(g, SRC, stride=GROUPS), :].astype(BF16)
            j = g % (BW // LANES)
            sgb[h * 4 + g // (BW // LANES), rows, pl.ds(j * LANES, LANES)] = part

    expert_row = lax.broadcasted_iota(jnp.int32, (SRC, TOK), 0)
    m0 = (ids[0:1, :] == expert_row).astype(F32)
    m1 = (ids[1:2, :] == expert_row).astype(F32)
    earlier = (
        lax.broadcasted_iota(jnp.int32, (TOK, TOK), 0) < lax.broadcasted_iota(jnp.int32, (TOK, TOK), 1)
    ).astype(F32).astype(BF16)
    before = dot((m0 + m1).astype(BF16), earlier, 1, 0)
    slot_row = lax.broadcasted_iota(jnp.int32, (SLOTS, TOK), 0)
    for k, m in ((0, m0), (1, m1)):
        position = jnp.sum(m * before, axis=0, keepdims=True).astype(jnp.int32)
        target = position * SRC + ids[k:k + 1, :]
        PT[:, k * TOK:(k + 1) * TOK] = (slot_row == target).astype(F32).astype(BF16)
        gcol[k] = jnp.broadcast_to(gates[k:k + 1, :], (TOK, TOK)).T

    def gate(k):
        return jnp.concatenate([gcol[k]] * (BW // LANES), axis=1)

    def gather(b, carry):
        cols = pl.ds(pl.multiple_of(b * BW, BW), BW)
        part = grad[:, cols].astype(F32)
        scaled = jnp.concatenate([(gate(0) * part).astype(BF16), (gate(1) * part).astype(BF16)], axis=0)
        stash(b, dot(PT[...], scaled, 1, 0))
        return carry

    gcopy.wait()
    for h in range(2):
        lax.fori_loop(4 * h, 4 * h + 4, gather, 0)
        spread(0, h)
        if h == 0:
            pl.semaphore_wait(barrier, 2 * (SIDE - 1) + NX)
        for ch in range(len(CHUNKS)):
            start_phase(0, 0, h, ch)
    wcopy.wait()

    def wmove(b, dev, i):
        return pltpu.make_async_remote_copy(
            src_ref=wf.at[b], dst_ref=wf.at[b], send_sem=wsend.at[i], recv_sem=wrecv.at[i],
            device_id=dev, device_id_type=MESH,
        )

    wx = [wmove(r, xdev((x + o) % NX), o) for o in (1, 3, 2)]
    for c in wx:
        c.start()
    wsib = [wmove(r, (sib, e), 4)]
    wsib[0].start()

    eye = (
        lax.broadcasted_iota(jnp.int32, (SLOTS, SLOTS), 0)
        == lax.broadcasted_iota(jnp.int32, (SLOTS, SLOTS), 1)
    ).astype(F32).astype(BF16)
    PP[...] = dot(PT[...], eye, 0, 0).astype(BF16)
    hcopy.wait()
    row = lax.broadcasted_iota(jnp.int32, (SLOTS, SLOTS), 0)
    col = lax.broadcasted_iota(jnp.int32, (SLOTS, SLOTS), 1)
    perm = (col == (row % SRC) * CAP + row // SRC).astype(F32).astype(BF16)
    hp[...] = dot(perm, hv[...], 1, 0).astype(BF16)
    hpT[...] = dot(hv[...], perm, 0, 1).astype(BF16)

    for h, ch in ORDER:
        wait_phase(0, 0, h, ch)
        start_phase(0, 1, h, ch)

    for c, o in zip(wx, (1, 3, 2)):
        c.wait()
        fwd = wmove(((x + NX - o) % NX) * 2 + core, (sib, e), 4 + o)
        fwd.start()
        wsib.append(fwd)
    for c in wsib:
        c.wait()

    def expert(b, carry):
        stash(b, dot(hp[...], wf[b], 1, 0))
        return carry

    for h in range(2):
        lax.fori_loop(4 * h, 4 * h + 4, expert, 0)
        spread(1, h)
        for ch in range(len(CHUNKS)):
            start_phase(1, 0, h, ch)

    def take_in(a, h, ch):
        wait_phase(a, 1, h, ch)

        def take(c, carry):
            collect(a, h, c)
            return carry

        lax.fori_loop(*CHUNKS[ch], take, 0)

    for h, ch in ORDER:
        take_in(0, h, ch)

    def dmove(src, dst, dev, i):
        return pltpu.make_async_remote_copy(
            src_ref=src, dst_ref=dst, send_sem=dsend.at[i], recv_sem=drecv.at[i],
            device_id=dev, device_id_type=MESH,
        )

    def block_grad(b):
        return dot(hpT[...], sgb[b], 1, 0)

    def for_sibling(i, carry):
        dws[i] = block_grad(i * 2 + 1 - core).astype(BF16)
        dmove(dws.at[i], sibr.at[i], (sib, e), i).start()
        return carry

    lax.fori_loop(0, NX, for_sibling, 0)

    def back(b, carry):
        hacc[...] += dot(sgb[b], wf[b], 1, 1)
        return carry

    hacc[...] = jnp.zeros_like(hacc)
    lax.fori_loop(0, REP, back, 0)
    hg_o[...] = dot(perm, hacc[...].astype(BF16), 0, 0).astype(BF16)

    def own_type(o, carry):
        t = (x + o) % NX
        dmove(dws.at[t], sibr.at[t], (sib, e), t).wait()
        xs[o] = (block_grad(t * 2 + core) + sibr[t].astype(F32)).astype(BF16)
        dmove(xs.at[o], xr.at[o], xdev(t), NX + o).start()
        return carry

    lax.fori_loop(1, NX, own_type, 0)
    dmove(dws.at[x], sibr.at[x], (sib, e), x).wait()
    acc[...] = block_grad(r) + sibr[x].astype(F32)

    for h, ch in ORDER:
        wait_phase(1, 0, h, ch)
        start_phase(1, 1, h, ch)

    for o in (1, 3, 2):
        dmove(xs.at[o], xr.at[o], xdev((x + o) % NX), NX + o).wait()
    dw_o[...] = (acc[...] + xr[1].astype(F32) + xr[2].astype(F32) + xr[3].astype(F32)).astype(BF16)

    gsum[...] = jnp.zeros_like(gsum)
    last = len(CHUNKS) - 1
    for h, ch in ORDER:
        take_in(1, h, ch)
        rows = slice(CHUNKS[ch][0] * SRC, CHUNKS[ch][1] * SRC)

        def combine(b, carry, ch=ch, rows=rows):
            picked = dot(PP[:, rows], sgb[b, rows], 1, 0)
            if ch > 0:
                picked += pacc[b]
            if ch < last:
                pacc[b] = picked
                return carry
            cols = pl.ds(pl.multiple_of(b * BW, BW), BW)
            part = grad[:, cols].astype(F32)
            p0, p1 = picked[:TOK], picked[TOK:]
            comb_o[:, cols] = (gate(0) * p0 + gate(1) * p1).astype(BF16)
            for k, p in ((0, p0), (1, p1)):
                q = part * p
                gsum[k] += (q[:, 0:LANES] + q[:, LANES:2 * LANES]) + (
                    q[:, 2 * LANES:3 * LANES] + q[:, 3 * LANES:]
                )
            return carry

        lax.fori_loop(4 * h, 4 * h + 4, combine, 0)
    for k in range(2):
        gg_o[k:k + 1, :] = jnp.sum(gsum[k].T, axis=0, keepdims=True)

    for a in range(2):
        for phase in range(2):
            for h in range(2):
                wait_sent(a, phase, h)


def deliver(*refs):
    sems = refs[-1]
    copies = [pltpu.make_async_copy(refs[i], refs[4 + i], sems.at[i]) for i in range(4)]
    for c in copies:
        c.start()
    for c in copies:
        c.wait()


def per_device(hidden, down_weight, grad_out, expert_ids, gate_weights):
    vmem = pl.BlockSpec(memory_space=pltpu.VMEM)
    hbm = pl.BlockSpec(memory_space=pl.ANY)
    dma = pltpu.SemaphoreType.DMA
    n = len(CHUNKS)
    a2a = pltpu.VMEM((2, 2, CAP, SIDE, SIDE, GROUPS, LANES), BF16)
    quarter = pltpu.VMEM((NX, FF, BW), BF16)
    held = pl.pallas_call(
        kernel,
        out_shape=(
            pltpu.VMEM((TOK, D), BF16),
            pltpu.VMEM((SLOTS, FF), BF16),
            pltpu.VMEM((FF, BW), BF16),
            pltpu.VMEM((2, TOK), F32),
        ),
        in_specs=[hbm, hbm, hbm, vmem, vmem],
        out_specs=(vmem,) * 4,
        scratch_shapes=[
            a2a, a2a, a2a,
            pltpu.VMEM((SLOTS * GROUPS, LANES), F32),
            pltpu.VMEM((REP, FF, BW), BF16),
            pltpu.VMEM((REP, SLOTS, BW), BF16),
            pltpu.VMEM((TOK, D), BF16),
            pltpu.VMEM((SLOTS, FF), BF16),
            pltpu.VMEM((SLOTS, FF), BF16),
            pltpu.VMEM((FF, SLOTS), BF16),
            pltpu.VMEM((SLOTS, 2 * TOK), BF16),
            pltpu.VMEM((2 * TOK, SLOTS), BF16),
            quarter, quarter, quarter, quarter,
            pltpu.VMEM((FF, BW), F32),
            pltpu.VMEM((SLOTS, FF), F32),
            pltpu.VMEM((2, TOK, LANES), F32),
            pltpu.VMEM((2, TOK, LANES), F32),
            pltpu.VMEM((REP, 2 * TOK, BW), F32),
            dma((2, 2, 2)), dma((2, 2, 2, n)), dma((2, 2, 2, n)),
            dma((8,)), dma((8,)), dma, dma, dma,
            dma((8,)), dma((8,)),
        ],
        compiler_params=pltpu.CompilerParams(
            collective_id=0, has_side_effects=True, vmem_limit_bytes=57 * 1024 * 1024
        ),
        cost_estimate=pl.CostEstimate(
            flops=7_000_000_000, bytes_accessed=5_000_000, transcendentals=0
        ),
    )(hidden[0, 0], down_weight[0], grad_out, expert_ids.T, gate_weights.T)
    combined, hidden_grad, weight_grad, gate_grad = pl.pallas_call(
        deliver,
        out_shape=(
            jax.ShapeDtypeStruct((TOK, D), BF16),
            jax.ShapeDtypeStruct((SLOTS, FF), BF16),
            jax.ShapeDtypeStruct((FF, BW), BF16),
            jax.ShapeDtypeStruct((2, TOK), F32),
        ),
        in_specs=[vmem] * 4,
        out_specs=(hbm,) * 4,
        scratch_shapes=[dma((4,))],
    )(*(pltpu.with_memory_space_constraint(a, pltpu.VMEM) for a in held))
    return combined, hidden_grad[None, None], weight_grad[None], gate_grad.T


def solution(mesh):
    return jax.shard_map(
        per_device,
        mesh=mesh,
        in_specs=(
            P("rep", "exp", None, None),
            P("exp", None, "rep"),
            P(("rep", "exp"), None),
            P(("rep", "exp"), None),
            P(("rep", "exp"), None),
        ),
        out_specs=(
            P(("rep", "exp"), None),
            P("rep", "exp", None, None),
            P("exp", None, "rep"),
            P(("rep", "exp"), None),
        ),
        check_vma=False,
    )
```
